256 devices in a mesh: seq: 32 (over y, z), tp: 8 (over x, core).
Axes of the slice: x: 4, y: 4, z: 8, core: 2. Of those that a mesh axis runs over, the one named last changes fastest.
Arguments:
- hidden: bfloat16 [16384, 8192], P('seq', 'tp'), may hold values from -6 to 6
- value_weight: bfloat16 [8192, 4096], P('seq', 'tp'), may hold values from -0.0625 to 0.0625
- gate: bfloat16 [16384, 4096], P('seq', 'tp'), may hold values from -6 to 6
- filters: bfloat16 [16384, 32], P('seq', 'tp'), may hold values from -1 to 1
- skip_gain: float32 [4096], P('tp'), may hold values from 0.5 to 1.5
Outputs:
- mixed: bfloat16 [16384, 4096], P('seq', 'tp')
The draws below stay inside these ranges and needn't reach their ends.
All inputs are finite; a program needn't handle non-finite values.
Results may differ from the reference program's by a relative error of at most 0.0051.
Values may be sent and summed in bfloat16 or wider, within the bound.
No kernel may reach another device: no remote copies, remote signals or barrier semaphores. Data moves between devices by JAX's collectives and lax.ppermute only.
A program may use at most 128 MiB of HBM per device.

```python
import jax
import jax.numpy as jnp
from jax import lax

D = 8192
CH = 4096
GROUP = 128
SEQUENCE_LENGTH = 16384
KERNEL_BANKS = 32


def draw_hidden(key, part):
    key = jax.random.fold_in(key, 11)
    feature_keys = jax.random.split(key, 2)
    noise = jax.random.normal(feature_keys[0], (SEQUENCE_LENGTH, D), jnp.float32)
    common = jnp.clip(jax.random.normal(feature_keys[1], (D,), jnp.float32), -3.0, 3.0)
    return jnp.clip(noise + common[None, :], -6.0, 6.0).astype(jnp.bfloat16)


def draw_filters(key, part):
    key = jax.random.fold_in(key, 7)
    filter_keys = jax.random.split(key, 7)
    moment_indices = jnp.arange(SEQUENCE_LENGTH, dtype=jnp.float32)[:, None]
    rough = jnp.clip(jax.random.normal(filter_keys[0], (SEQUENCE_LENGTH, KERNEL_BANKS), jnp.float32), -5.0, 5.0)
    slow_share = 0.5
    slow = jax.random.uniform(filter_keys[1], (KERNEL_BANKS,), jnp.float32) < slow_share
    long_reach = SEQUENCE_LENGTH * jax.random.uniform(filter_keys[2], (KERNEL_BANKS,), jnp.float32, 0.5, 4.0)
    short_reach = jax.random.uniform(filter_keys[3], (KERNEL_BANKS,), jnp.float32, 30.0, 300.0)
    reach = jnp.where(slow, long_reach, short_reach)
    scale_taps = 1.0 / jnp.sqrt(jnp.minimum(reach, SEQUENCE_LENGTH * 1.0))
    kernel_pulses = jax.random.randint(filter_keys[4], (2, KERNEL_BANKS), 0, SEQUENCE_LENGTH).astype(jnp.float32)
    damping_speeds = jnp.where(moment_indices >= kernel_pulses[0][None, :], 0.6, 1.0) * jnp.where(moment_indices >= kernel_pulses[1][None, :], 0.7, 1.0)
    head = rough * scale_taps[None, :] * jnp.exp(-moment_indices / reach[None, :]) * damping_speeds
    cutoff = jax.random.randint(filter_keys[5], (KERNEL_BANKS,), 400, 512).astype(jnp.float32)
    tail_sign = jnp.where(jax.random.uniform(filter_keys[6], (KERNEL_BANKS,), jnp.float32) < 0.5, -1.0, 1.0)
    short_taps = jnp.where(moment_indices < cutoff[None, :], head, 3e-06 * tail_sign[None, :])
    return jnp.where(slow[None, :], head, short_taps).astype(jnp.bfloat16)


def level_of(stream_key, shape, cuts, smallest, high):
    def one(dim, parts):
        draws = jax.random.uniform(jax.random.fold_in(jax.random.fold_in(stream_key, 6), dim), (parts,), jnp.float32, smallest / len(cuts), high / len(cuts))
        return jnp.repeat(jnp.exp(draws), shape[dim] // parts).reshape((-1,) + (1,) * (len(shape) - dim - 1))

    gain = one(*cuts[0])
    for cut in cuts[1:]:
        gain = gain * one(*cut)
    return gain


def scatter_about(rng, dims, spread, limit, pieces=(), kind=jnp.bfloat16):
    loudness = level_of(rng, dims, pieces, -0.22, 0.18) if pieces else 1.0
    array = jax.random.normal(rng, dims, jnp.float32) * spread * loudness
    return jnp.minimum(jnp.maximum(array, -limit), limit).astype(kind)


def setup_inputs(seed: int = 0) -> dict:
    seeds = jax.random.split(jax.random.key(seed), 6)
    hidden = draw_hidden(jax.random.fold_in(seeds[5], 71), 0)
    value_weight = scatter_about(seeds[1], (D, CH), D ** -0.5, 0.0625, ((0, 32), (1, 8)))
    gate = scatter_about(seeds[2], (SEQUENCE_LENGTH, CH), 1.0, 6.0, ((0, 32), (1, 8)))
    filters = draw_filters(jax.random.fold_in(seeds[5], 71), 0)
    skip_gain = jnp.clip(0.5 + 1.0 * jax.random.uniform(seeds[4], (CH,), jnp.float32) ** level_of(seeds[4], (CH,), ((0, 8),), -0.2, 0.2), 0.5, 1.5)
    return {"hidden": hidden, "value_weight": value_weight, "gate": gate, "filters": filters, "skip_gain": skip_gain}


def reference(hidden, value_weight, gate, filters, skip_gain):
    length = hidden.shape[0]

    def one_group(group_index):
        start = (group_index * GROUP).astype(jnp.int32)
        weights = lax.dynamic_slice_in_dim(value_weight, start, GROUP, 1)
        value = jnp.dot(hidden, weights, preferred_element_type=jnp.float32).astype(jnp.bfloat16)
        signal = value.astype(jnp.float32)
        taps = lax.dynamic_index_in_dim(filters, group_index, 1, keepdims=False).astype(jnp.float32)
        spectrum = jnp.fft.rfft(signal, n=2 * length, axis=0) * jnp.fft.rfft(taps, n=2 * length)[:, None]
        conv = jnp.fft.irfft(spectrum, n=2 * length, axis=0)[:length]
        gates = lax.dynamic_slice_in_dim(gate, start, GROUP, 1).astype(jnp.float32)
        gains = lax.dynamic_slice_in_dim(skip_gain, start, GROUP, 0)
        return (gates * (conv + gains[None, :] * signal)).astype(jnp.bfloat16)

    blocks = lax.map(one_group, jnp.arange(KERNEL_BANKS, dtype=jnp.int32))
    return jnp.transpose(blocks, (1, 0, 2)).reshape(length, KERNEL_BANKS * GROUP)
```

```python
import functools

import jax
import jax.numpy as jnp
from jax import lax
from jax.experimental import pallas as pl
from jax.experimental.pallas import tpu as pltpu
from jax.sharding import PartitionSpec as P

NY, NZ = 4, 8
FIRST = 112
TAP_ROWS = 16
WHOLE_VMEM = 60 * 1000 * 1000
VMEM_LIMIT = 16 * 1024 * 1024


def take_from(array, dy, dz):
    pairs = [
        (((y + dy) % NY) * NZ + (z + dz) % NZ, y * NZ + z) for y in range(NY) for z in range(NZ)
    ]
    return lax.ppermute(array, "seq", pairs)


def gather_weight(weight, filters):
    taps = jnp.tile(filters.T, (TAP_ROWS // filters.shape[1], 1))
    first = jnp.concatenate([weight[:FIRST], taps], axis=0)
    second = weight[FIRST:]

    def halves(one, other, dy, dz):
        half = one.shape[0] // 2
        return take_from(one[:half], dy, dz), take_from(other[half:], -dy, -dz)

    line = {0: first}
    up, down = take_from(second, 1, 0), take_from(second, -1, 0)
    for k in (1, 2, 3):
        line[k] = take_from(line[k - 1], 0, 1)
        line[-k] = take_from(line[1 - k], 0, -1)
    far = jnp.concatenate(halves(up, down, 1, 0), axis=0)
    column = jnp.stack([second, up, far, down])
    column, line[3], line[-3] = lax.optimization_barrier((column, line[3], line[-3]))
    line[4] = jnp.concatenate(halves(line[3], line[-3], 0, 1), axis=0)
    mine = jnp.stack([line[k] for k in (0, 1, 2, 3, 4, -3, -2, -1)])
    above, below = take_from(mine, 1, 0), take_from(mine, -1, 0)
    firsts = [mine, above, below, *halves(above, below, 1, 0)]
    ring = {0: column}
    for k in (1, 2, 3):
        ring[k] = take_from(ring[k - 1], 0, 1)
        ring[-k] = take_from(ring[1 - k], 0, -1)
    seconds = [ring[k] for k in (0, 1, 2, 3, -3, -2, -1)] + list(halves(ring[3], ring[-3], 0, 1))
    across = jnp.concatenate([firsts[3][:, FIRST:], firsts[4][:, FIRST:]], axis=0)
    taps = jnp.stack([mine[:, FIRST:], above[:, FIRST:], across, below[:, FIRST:]])
    return firsts, seconds, taps


def sources_of(dy, dz):
    one = (3 + dz // 4, dz % 4) if dy == 2 else ({0: 0, 1: 1, 3: 2}[dy], dz)
    other = (12 + dy // 2, dy % 2) if dz == 4 else (5 + (dz if dz < 4 else dz - 1), dy)
    return one, other


def project_kernel(steps, names, last, *refs):
    place, hidden_source = refs[:2]
    arrays = dict(zip(names, refs[2 : 2 + len(names)], strict=True))
    refs = refs[2 + len(names) :]
    before = None
    if last:
        before, refs = refs[0], refs[1:]
    out, hidden, weight, sem = refs
    y, z = place[0], place[1]
    copies = []
    for count, step in enumerate(steps):
        started = []
        for n, (dy, dz) in enumerate(step):
            row = (sum(len(s) for s in steps[:count]) + n) * 256
            block = lax.rem(y + dy, NY) * NZ + lax.rem(z + dz, NZ)
            pairs = [
                (
                    hidden_source.at[:, pl.ds(pl.multiple_of(block * 256, 256), 256)],
                    hidden.at[:, row : row + 256],
                )
            ]
            for (name, at), lo, hi in zip(sources_of(dy, dz), (0, FIRST), (FIRST, 256), strict=True):
                target = weight.at[row + lo : row + hi, :]
                pairs.append((arrays[name].at[at, 0 : hi - lo, :], target))
            for k, (source, target) in enumerate(pairs):
                copy = pltpu.make_async_copy(source, target, sem.at[row // 256, k])
                copy.start()
                started.append(copy)
        copies.append(started)
    total = before[...] if last else jnp.zeros((512, 512), jnp.float32)
    row = 0
    for step, started in zip(steps, copies, strict=True):
        for copy in started:
            copy.wait()
        rows = slice(row, row + 256 * len(step))
        total += jnp.dot(hidden[:, rows], weight[rows, :], preferred_element_type=jnp.float32)
        row += 256 * len(step)
    if last:
        out[...] = total.T.reshape(32, 16, 512).astype(jnp.bfloat16)
    else:
        out[...] = total


def project(place, hidden, pieces, steps, before=None):
    last = before is not None
    names = sorted(
        {name for step in steps for at in step for name, _ in sources_of(*at)}
    )
    count = sum(len(step) for step in steps)
    shape = (
        jax.ShapeDtypeStruct((32, 16, 512), jnp.bfloat16)
        if last
        else jax.ShapeDtypeStruct((512, 512), jnp.float32)
    )
    whole = pl.BlockSpec(memory_space=pltpu.VMEM)
    apart = pl.BlockSpec(memory_space=pl.ANY)
    return pl.pallas_call(
        functools.partial(project_kernel, steps, names, last),
        out_shape=shape,
        in_specs=[pl.BlockSpec(memory_space=pltpu.SMEM)]
        + [apart] * (1 + len(names))
        + [whole] * last,
        out_specs=whole,
        scratch_shapes=[
            pltpu.VMEM((512, 256 * count), jnp.bfloat16),
            pltpu.VMEM((256 * count, 512), jnp.bfloat16),
            pltpu.SemaphoreType.DMA((count, 3)),
        ],
        compiler_params=pltpu.CompilerParams(vmem_limit_bytes=WHOLE_VMEM),
        cost_estimate=pl.CostEstimate(
            flops=2 * 512 * 512 * 256 * count,
            bytes_accessed=count * 512 * 1024,
            transcendentals=0,
        ),
        name="project_last" if last else "project_early",
    )(place, hidden, *[pieces[name] for name in names], *([before] if last else []))


EARLY = [[(dy, dz) for dz in dzs] for dy in (0, 1, 3) for dzs in ((0, 1, 2, 3), (5, 6, 7))]
LATE = [
    [(2, 0), (2, 1), (2, 2), (2, 3)],
    [(0, 4), (1, 4), (3, 4), (2, 4)],
    [(2, 5), (2, 6), (2, 7)],
]


def strip_kernel(place, taps, out):
    rows, step = 256, 512
    y, z, which = place[0], place[1], place[2]
    pick = lax.broadcasted_iota(jnp.int32, (TAP_ROWS, step), 0) == which

    def chunk(i, before):
        dy = lax.rem(lax.div(i, NZ) - y + NY, NY)
        dz = lax.rem(lax.rem(i, NZ) - z + NZ, NZ)
        held = taps[dy, dz].astype(jnp.float32)
        block = jnp.sum(jnp.where(pick, held, 0.0), axis=0, keepdims=True)
        window = jnp.concatenate([before, block], axis=1)
        window = jnp.broadcast_to(window, (rows, step + rows))
        rolled = pltpu.roll(window, 0, 1, stride=1, stride_axis=0)
        out[:, pl.ds(pl.multiple_of(i * step, step), step)] = rolled[:, rows:].astype(jnp.bfloat16)
        return block[:, step - rows :]

    lax.fori_loop(0, out.shape[1] // step, chunk, jnp.zeros((1, rows), jnp.float32))


def strip(place, taps):
    vmem = pl.BlockSpec(memory_space=pltpu.VMEM)
    return pl.pallas_call(
        strip_kernel,
        out_shape=jax.ShapeDtypeStruct((256, 16384), jnp.bfloat16),
        in_specs=[pl.BlockSpec(memory_space=pltpu.SMEM), vmem],
        out_specs=vmem,
        compiler_params=pltpu.CompilerParams(vmem_limit_bytes=VMEM_LIMIT),
        cost_estimate=pl.CostEstimate(flops=10 << 20, bytes_accessed=8 << 20, transcendentals=0),
        name="strip",
    )(place, taps)


def conv_kernel(value, strip_ref, out, stacked, total):
    for e in range(4):
        for b in range(64):
            rows = slice(16 * b, 16 * b + 16)
            cols = slice(256 * e, 256 * e + 256)
            if b - e < 0:
                stacked[rows, cols] = jnp.zeros((16, 256), jnp.bfloat16)
            else:
                j, m = divmod(b - e, 2)
                stacked[rows, cols] = value[j, :, 256 * m : 256 * m + 256]
    for g in range(16):
        taps = jnp.concatenate(
            [strip_ref[:, 256 * (4 * g + e) : 256 * (4 * g + e + 1)] for e in range(4)], axis=0
        )
        term = jnp.dot(stacked[: 1024 - 64 * g], taps, preferred_element_type=jnp.float32)
        if g == 0:
            total[...] = term
        else:
            total[64 * g :] += term
    for b in range(64):
        j, m = divmod(b, 2)
        out[j, :, 256 * m : 256 * m + 256] = total[16 * b : 16 * b + 16].astype(jnp.bfloat16)


def convolve(value, taps_strip):
    vmem = pl.BlockSpec(memory_space=pltpu.VMEM)
    return pl.pallas_call(
        conv_kernel,
        out_shape=jax.ShapeDtypeStruct((32, 16, 512), jnp.bfloat16),
        in_specs=[vmem, vmem],
        out_specs=vmem,
        scratch_shapes=[
            pltpu.VMEM((1024, 1024), jnp.bfloat16),
            pltpu.VMEM((1024, 256), jnp.float32),
        ],
        compiler_params=pltpu.CompilerParams(vmem_limit_bytes=VMEM_LIMIT),
        cost_estimate=pl.CostEstimate(
            flops=4_500_000_000, bytes_accessed=10 << 20, transcendentals=0
        ),
        name="convolve",
    )(value, taps_strip)


def mix_kernel(conv, value, gain, gate, out):
    column = jnp.transpose(jnp.broadcast_to(gain[...], (8, gain.shape[1])))[:, :1]
    total = conv[...].astype(jnp.float32) + column * value[...].astype(jnp.float32)
    out[...] = (gate[...].astype(jnp.float32) * total.T).astype(jnp.bfloat16)


def mix(conv, value, gain, gate):
    return pl.pallas_call(
        mix_kernel,
        out_shape=jax.ShapeDtypeStruct((512, 512), jnp.bfloat16),
        grid=(4,),
        in_specs=[
            pl.BlockSpec((128, 512), lambda i: (i, 0)),
            pl.BlockSpec((128, 512), lambda i: (i, 0)),
            pl.BlockSpec((1, 128), lambda i: (0, i)),
            pl.BlockSpec((512, 128), lambda i: (0, i)),
        ],
        out_specs=pl.BlockSpec((512, 128), lambda i: (0, i)),
        compiler_params=pltpu.CompilerParams(vmem_limit_bytes=VMEM_LIMIT),
        name="mix",
    )(conv, value, gain, gate)


def on_device(hidden, value_weight, gate, filters, skip_gain):
    index = lax.axis_index("seq")
    place = jnp.stack([index // NZ, index % NZ, index // 8]).astype(jnp.int32)
    whole = lax.all_gather(hidden, "tp", axis=1, tiled=True)
    firsts, seconds, taps = gather_weight(value_weight, filters)
    pieces = [*firsts, *seconds]
    early = project(place, whole, pieces, EARLY)
    value = project(place, whole, pieces, LATE, early)
    value, taps = lax.optimization_barrier((value, taps))
    taps_strip = strip(place, taps)
    value, taps_strip = lax.optimization_barrier((value, taps_strip))
    moved = lax.all_to_all(value, "seq", split_axis=0, concat_axis=0, tiled=True)
    conv = convolve(moved, taps_strip)
    arrived = lax.all_to_all(conv, "seq", split_axis=0, concat_axis=0, tiled=True)
    return mix(arrived.reshape(512, 512), value.reshape(512, 512), skip_gain[None], gate)


def solution(mesh):
    in_specs = (P("seq", "tp"), P("seq", "tp"), P("seq", "tp"), P("seq", "tp"), P("tp"))
    out_specs = P("seq", "tp")
    return jax.shard_map(
        on_device, mesh=mesh, in_specs=in_specs, out_specs=out_specs, check_vma=False
    )
```

```python
import functools

import jax
import jax.numpy as jnp
from jax import lax
from jax.experimental import pallas as pl
from jax.experimental.pallas import tpu as pltpu
from jax.sharding import PartitionSpec as P

NY, NZ = 4, 8
FIRST = 128
TAP_ROWS = 16
VMEM_LIMIT = 16 * 1024 * 1024


def take_from(array, dy, dz):
    pairs = [
        (((y + dy) % NY) * NZ + (z + dz) % NZ, y * NZ + z) for y in range(NY) for z in range(NZ)
    ]
    return lax.ppermute(array, "seq", pairs)


def project_kernel(parts, first, last, place, hidden, *refs):
    refs = list(refs)
    out = refs.pop()
    total = jnp.zeros((512, 512), jnp.float32) if first else refs.pop()[...]
    y, z = place[0], place[1]
    pieces = []
    for ref, part in zip(refs, parts, strict=True):
        for at, (dy, dz, second) in enumerate(part):
            block = lax.rem(y + dy, NY) * NZ + lax.rem(z + dz, NZ)
            start = pl.multiple_of(block * 256 + FIRST * second, FIRST)
            pieces.append((start, ref, at))
    for n in range(0, len(pieces), 8):
        group = pieces[n : n + 8]
        left = [hidden[:, pl.ds(start, FIRST)] for start, _, _ in group]
        right = [ref[at, 0:FIRST, :] for _, ref, at in group]
        total += jnp.dot(
            jnp.concatenate(left, axis=1),
            jnp.concatenate(right, axis=0),
            preferred_element_type=jnp.float32,
        )
    out[...] = total.T.reshape(32, 16, 512).astype(jnp.bfloat16) if last else total


def project(place, hidden, held, before=None, last=False):
    arrays = [array for array, _ in held]
    parts = [part for _, part in held]
    count = sum(len(part) for part in parts)
    shape = (
        jax.ShapeDtypeStruct((32, 16, 512), jnp.bfloat16)
        if last
        else jax.ShapeDtypeStruct((512, 512), jnp.float32)
    )
    vmem = pl.BlockSpec(memory_space=pltpu.VMEM)
    extra = [] if before is None else [before]
    return pl.pallas_call(
        functools.partial(project_kernel, parts, before is None, last),
        out_shape=shape,
        in_specs=[pl.BlockSpec(memory_space=pltpu.SMEM)] + [vmem] * (1 + len(arrays) + len(extra)),
        out_specs=vmem,
        compiler_params=pltpu.CompilerParams(vmem_limit_bytes=VMEM_LIMIT),
        cost_estimate=pl.CostEstimate(
            flops=2 * 512 * 512 * FIRST * count,
            bytes_accessed=count * 256 * 1024,
            transcendentals=0,
        ),
        name=f"project_{count}",
    )(place, hidden, *arrays, *extra)


def halves(one, other, dy, dz):
    half = one.shape[0] // 2
    return take_from(one[:half], dy, dz), take_from(other[half:], -dy, -dz)


def gather_and_project(place, hidden, weight, filters):
    taps = jnp.tile(filters.T, (TAP_ROWS // filters.shape[1], 1))
    first = jnp.concatenate([weight[:FIRST], taps], axis=0)
    second = weight[FIRST:]
    line = {0: first, 1: take_from(first, 0, 1), -1: take_from(first, 0, -1)}
    column = jnp.stack([second, *(take_from(second, k, 0) for k in (1, 2, 3))])
    line[2], line[-2] = take_from(line[1], 0, 1), take_from(line[-1], 0, -1)
    line[2], line[-2], column = lax.optimization_barrier((line[2], line[-2], column))
    line[3], line[-3] = take_from(line[2], 0, 1), take_from(line[-2], 0, -1)
    ring = {0: column, 1: take_from(column, 0, 1), -1: take_from(column, 0, -1)}
    line[3], line[-3], ring[1], ring[-1] = lax.optimization_barrier(
        (line[3], line[-3], ring[1], ring[-1])
    )
    line[4] = jnp.concatenate(halves(line[3], line[-3], 0, 1), axis=0)
    mine = jnp.stack([line[k] for k in (0, 1, 2, 3, 4, -3, -2, -1)])
    above, below = take_from(mine, 1, 0), take_from(mine, -1, 0)

    def row(dy, start=0, stop=NZ):
        return [(dy, dz, 0) for dz in range(start, stop)]

    def stack(dz, start=0, stop=NY):
        return [(dy, dz % NZ, 1) for dy in range(start, stop)]

    ring[2], ring[-2] = take_from(ring[1], 0, 1), take_from(ring[-1], 0, -1)
    held = [(mine, row(0))] + [(ring[k], stack(k)) for k in (0, 1, -1)]
    total = project(place, hidden, held)
    total, ring[2], ring[-2] = lax.optimization_barrier((total, ring[2], ring[-2]))
    ring[3], ring[-3] = take_from(ring[2], 0, 1), take_from(ring[-2], 0, -1)
    total = project(place, hidden, [(ring[k], stack(k)) for k in (2, -2)], total)
    total, above, below = lax.optimization_barrier((total, above, below))
    across = halves(above, below, 1, 0)
    total = project(place, hidden, [(above, row(1)), (below, row(3))], total)
    total, ring[3], ring[-3] = lax.optimization_barrier((total, ring[3], ring[-3]))
    ends = halves(ring[3], ring[-3], 0, 1)
    total = project(place, hidden, [(ring[k], stack(k)) for k in (3, -3)], total)
    held = [(across[0], row(2, 0, 4)), (across[1], row(2, 4, 8))]
    held += [(ends[0], stack(4, 0, 2)), (ends[1], stack(4, 2, 4))]
    value = project(place, hidden, held, total, last=True)
    across = jnp.concatenate([part[:, FIRST:] for part in across], axis=0)
    taps = jnp.stack([mine[:, FIRST:], above[:, FIRST:], across, below[:, FIRST:]])
    return value, taps


def strip_kernel(place, taps, out):
    rows, step = 256, 512
    y, z, which = place[0], place[1], place[2]
    pick = lax.broadcasted_iota(jnp.int32, (TAP_ROWS, step), 0) == which

    def chunk(i, before):
        dy = lax.rem(lax.div(i, NZ) - y + NY, NY)
        dz = lax.rem(lax.rem(i, NZ) - z + NZ, NZ)
        held = taps[dy, dz].astype(jnp.float32)
        block = jnp.sum(jnp.where(pick, held, 0.0), axis=0, keepdims=True)
        window = jnp.concatenate([before, block], axis=1)
        window = jnp.broadcast_to(window, (rows, step + rows))
        rolled = pltpu.roll(window, 0, 1, stride=1, stride_axis=0)
        out[:, pl.ds(pl.multiple_of(i * step, step), step)] = rolled[:, rows:].astype(jnp.bfloat16)
        return block[:, step - rows :]

    lax.fori_loop(0, out.shape[1] // step, chunk, jnp.zeros((1, rows), jnp.float32))


def strip(place, taps):
    vmem = pl.BlockSpec(memory_space=pltpu.VMEM)
    return pl.pallas_call(
        strip_kernel,
        out_shape=jax.ShapeDtypeStruct((256, 16384), jnp.bfloat16),
        in_specs=[pl.BlockSpec(memory_space=pltpu.SMEM), vmem],
        out_specs=vmem,
        compiler_params=pltpu.CompilerParams(vmem_limit_bytes=VMEM_LIMIT),
        cost_estimate=pl.CostEstimate(flops=10 << 20, bytes_accessed=8 << 20, transcendentals=0),
        name="strip",
    )(place, taps)


def conv_kernel(value, strip_ref, out, stacked, total):
    for e in range(4):
        for b in range(64):
            rows = slice(16 * b, 16 * b + 16)
            cols = slice(256 * e, 256 * e + 256)
            if b - e < 0:
                stacked[rows, cols] = jnp.zeros((16, 256), jnp.bfloat16)
            else:
                j, m = divmod(b - e, 2)
                stacked[rows, cols] = value[j, :, 256 * m : 256 * m + 256]
    for g in range(16):
        taps = jnp.concatenate(
            [strip_ref[:, 256 * (4 * g + e) : 256 * (4 * g + e + 1)] for e in range(4)], axis=0
        )
        term = jnp.dot(stacked[: 1024 - 64 * g], taps, preferred_element_type=jnp.float32)
        if g == 0:
            total[...] = term
        else:
            total[64 * g :] += term
    for b in range(64):
        j, m = divmod(b, 2)
        out[j, :, 256 * m : 256 * m + 256] = total[16 * b : 16 * b + 16].astype(jnp.bfloat16)


def convolve(value, taps_strip):
    vmem = pl.BlockSpec(memory_space=pltpu.VMEM)
    return pl.pallas_call(
        conv_kernel,
        out_shape=jax.ShapeDtypeStruct((32, 16, 512), jnp.bfloat16),
        in_specs=[vmem, vmem],
        out_specs=vmem,
        scratch_shapes=[
            pltpu.VMEM((1024, 1024), jnp.bfloat16),
            pltpu.VMEM((1024, 256), jnp.float32),
        ],
        compiler_params=pltpu.CompilerParams(vmem_limit_bytes=VMEM_LIMIT),
        cost_estimate=pl.CostEstimate(
            flops=4_500_000_000, bytes_accessed=10 << 20, transcendentals=0
        ),
        name="convolve",
    )(value, taps_strip)


def mix_kernel(conv, value, gain, gate, out):
    column = jnp.transpose(jnp.broadcast_to(gain[...], (8, gain.shape[1])))[:, :1]
    total = conv[...].astype(jnp.float32) + column * value[...].astype(jnp.float32)
    out[...] = (gate[...].astype(jnp.float32) * total.T).astype(jnp.bfloat16)


def mix(conv, value, gain, gate):
    return pl.pallas_call(
        mix_kernel,
        out_shape=jax.ShapeDtypeStruct((512, 512), jnp.bfloat16),
        grid=(4,),
        in_specs=[
            pl.BlockSpec((128, 512), lambda i: (i, 0)),
            pl.BlockSpec((128, 512), lambda i: (i, 0)),
            pl.BlockSpec((1, 128), lambda i: (0, i)),
            pl.BlockSpec((512, 128), lambda i: (0, i)),
        ],
        out_specs=pl.BlockSpec((512, 128), lambda i: (0, i)),
        compiler_params=pltpu.CompilerParams(vmem_limit_bytes=VMEM_LIMIT),
        name="mix",
    )(conv, value, gain, gate)


def on_device(hidden, value_weight, gate, filters, skip_gain):
    index = lax.axis_index("seq")
    place = jnp.stack([index // NZ, index % NZ, index // 8]).astype(jnp.int32)
    whole = lax.all_gather(hidden, "tp", axis=1, tiled=True)
    value, taps = gather_and_project(place, whole, value_weight, filters)
    taps_strip = strip(place, taps)
    value, taps_strip = lax.optimization_barrier((value, taps_strip))
    moved = lax.all_to_all(value, "seq", split_axis=0, concat_axis=0, tiled=True)
    conv = convolve(moved, taps_strip)
    arrived = lax.all_to_all(conv, "seq", split_axis=0, concat_axis=0, tiled=True)
    return mix(arrived.reshape(512, 512), value.reshape(512, 512), skip_gain[None], gate)


def solution(mesh):
    in_specs = (P("seq", "tp"), P("seq", "tp"), P("seq", "tp"), P("seq", "tp"), P("tp"))
    out_specs = P("seq", "tp")
    return jax.shard_map(
        on_device, mesh=mesh, in_specs=in_specs, out_specs=out_specs, check_vma=False
    )
```

```python
import functools

import jax
import jax.numpy as jnp
from jax import lax
from jax.experimental import pallas as pl
from jax.experimental.pallas import tpu as pltpu
from jax.sharding import PartitionSpec as P

NY, NZ = 4, 8
FIRST = 128
TAP_ROWS = 8
VMEM_LIMIT = 16 * 1024 * 1024


def take_from(array, dy, dz):
    pairs = [
        (((y + dy) % NY) * NZ + (z + dz) % NZ, y * NZ + z) for y in range(NY) for z in range(NZ)
    ]
    return lax.ppermute(array, "seq", pairs)


def starts_kernel(place, out):
    for dy in range(NY):
        for dz in range(NZ):
            block = lax.rem(place[0] + dy, NY) * NZ + lax.rem(place[1] + dz, NZ)
            out[dy * NZ + dz] = block * 2 * FIRST


def starts_of(place):
    return pl.pallas_call(
        starts_kernel,
        out_shape=jax.ShapeDtypeStruct((NY * NZ,), jnp.int32),
        in_specs=[pl.BlockSpec(memory_space=pltpu.SMEM)],
        out_specs=pl.BlockSpec(memory_space=pltpu.SMEM),
        compiler_params=pltpu.CompilerParams(vmem_limit_bytes=VMEM_LIMIT),
        cost_estimate=pl.CostEstimate(
            flops=8_000_000_000, bytes_accessed=1 << 20, transcendentals=0
        ),
        name="starts",
    )(place)


def project_kernel(parts, first, last, starts, hidden, *refs):
    refs = list(refs)
    out = refs.pop()
    total = jnp.zeros((512, 512), jnp.float32) if first else refs.pop()[...]
    pieces = []
    for ref, part in zip(refs, parts, strict=True):
        for at, (dy, dz, second) in enumerate(part):
            start = pl.multiple_of(starts[dy * NZ + dz] + FIRST * second, FIRST)
            pieces.append((start, ref, at))
    for n in range(0, len(pieces), 8):
        group = pieces[n : n + 8]
        left = [hidden[:, pl.ds(start, FIRST)] for start, _, _ in group]
        right = [ref[at, 0:FIRST, :] for _, ref, at in group]
        total += jnp.dot(
            jnp.concatenate(left, axis=1),
            jnp.concatenate(right, axis=0),
            preferred_element_type=jnp.float32,
        )
    out[...] = total.T.reshape(32, 16, 512).astype(jnp.bfloat16) if last else total


def project(starts, hidden, held, before=None, last=False):
    arrays = [array for array, _ in held]
    parts = [part for _, part in held]
    count = sum(len(part) for part in parts)
    shape = (
        jax.ShapeDtypeStruct((32, 16, 512), jnp.bfloat16)
        if last
        else jax.ShapeDtypeStruct((512, 512), jnp.float32)
    )
    vmem = pl.BlockSpec(memory_space=pltpu.VMEM)
    extra = [] if before is None else [before]
    return pl.pallas_call(
        functools.partial(project_kernel, parts, before is None, last),
        out_shape=shape,
        in_specs=[pl.BlockSpec(memory_space=pltpu.SMEM)] + [vmem] * (1 + len(arrays) + len(extra)),
        out_specs=vmem,
        compiler_params=pltpu.CompilerParams(vmem_limit_bytes=VMEM_LIMIT),
        cost_estimate=pl.CostEstimate(
            flops=2 * 512 * 512 * FIRST * count,
            bytes_accessed=count * 256 * 1024,
            transcendentals=0,
        ),
        name=f"project_{count}",
    )(starts, hidden, *arrays, *extra)


def halves(one, other, dy, dz):
    half = one.shape[0] // 2
    return take_from(one[:half], dy, dz), take_from(other[half:], -dy, -dz)


def gather_and_project(place, hidden, weight, filters):
    taps = jnp.tile(filters.T, (TAP_ROWS // filters.shape[1], 1))
    first = jnp.concatenate([weight[:FIRST], taps], axis=0)
    second = weight[FIRST:]
    line = {0: first, 1: take_from(first, 0, 1), -1: take_from(first, 0, -1)}
    column = jnp.stack([second, *(take_from(second, k, 0) for k in (1, 2, 3))])
    line[2], line[-2] = take_from(line[1], 0, 1), take_from(line[-1], 0, -1)
    line[3], line[-3] = take_from(line[2], 0, 1), take_from(line[-2], 0, -1)
    ring = {0: column, 1: take_from(column, 0, 1), -1: take_from(column, 0, -1)}
    line[3], line[-3], ring[1], ring[-1] = lax.optimization_barrier(
        (line[3], line[-3], ring[1], ring[-1])
    )
    line[4] = jnp.concatenate(halves(line[3], line[-3], 0, 1), axis=0)
    mine = jnp.stack([line[k] for k in (0, 1, 2, 3, 4, -3, -2, -1)])
    above, below = take_from(mine, 1, 0), take_from(mine, -1, 0)

    def row(dy, start=0, stop=NZ):
        return [(dy, dz, 0) for dz in range(start, stop)]

    def stack(dz, start=0, stop=NY):
        return [(dy, dz % NZ, 1) for dy in range(start, stop)]

    ring[2], ring[-2] = take_from(ring[1], 0, 1), take_from(ring[-1], 0, -1)
    place, ring[2], ring[-2] = lax.optimization_barrier((place, ring[2], ring[-2]))
    starts = starts_of(place)
    starts, ring[2], ring[-2] = lax.optimization_barrier((starts, ring[2], ring[-2]))
    held = [(mine, row(0))] + [(ring[k], stack(k)) for k in (0, 1, -1)]
    total = project(starts, hidden, held)
    ring[3], ring[-3] = take_from(ring[2], 0, 1), take_from(ring[-2], 0, -1)
    total = project(starts, hidden, [(ring[k], stack(k)) for k in (2, -2)], total)
    total, above, below = lax.optimization_barrier((total, above, below))
    across = halves(above, below, 1, 0)
    total = project(starts, hidden, [(above, row(1)), (below, row(3))], total)
    total, ring[3], ring[-3] = lax.optimization_barrier((total, ring[3], ring[-3]))
    ends = halves(ring[3], ring[-3], 0, 1)
    total = project(starts, hidden, [(ring[k], stack(k)) for k in (3, -3)], total)
    held = [(across[0], row(2, 0, 4)), (across[1], row(2, 4, 8))]
    held += [(ends[0], stack(4, 0, 2)), (ends[1], stack(4, 2, 4))]
    value = project(starts, hidden, held, total, last=True)
    across = jnp.concatenate([part[:, FIRST:] for part in across], axis=0)
    taps = jnp.stack([mine[:, FIRST:], above[:, FIRST:], across, below[:, FIRST:]])
    return value, taps


def strip_kernel(place, taps, out):
    rows, step = 256, 512
    y, z = place[0], place[1]

    def block(i):
        dy = lax.rem(lax.div(i, NZ) - y + NY, NY)
        dz = lax.rem(lax.rem(i, NZ) - z + NZ, NZ)
        return taps[dy, dz]

    def chunk(i, carry):
        before = jnp.where(i == 0, 0.0, block(jnp.maximum(i - 1, 0))[:, step - rows :])
        window = jnp.concatenate([before, block(i)], axis=1)
        window = jnp.broadcast_to(window, (rows, step + rows))
        rolled = pltpu.roll(window, 0, 1, stride=1, stride_axis=0)
        out[:, pl.ds(pl.multiple_of(i * step, step), step)] = rolled[:, rows:].astype(jnp.bfloat16)
        return carry

    lax.fori_loop(0, out.shape[1] // step, chunk, 0)


def strip(place, taps):
    vmem = pl.BlockSpec(memory_space=pltpu.VMEM)
    return pl.pallas_call(
        strip_kernel,
        out_shape=jax.ShapeDtypeStruct((256, 16384), jnp.bfloat16),
        in_specs=[pl.BlockSpec(memory_space=pltpu.SMEM), vmem],
        out_specs=vmem,
        compiler_params=pltpu.CompilerParams(vmem_limit_bytes=VMEM_LIMIT),
        cost_estimate=pl.CostEstimate(flops=10 << 20, bytes_accessed=8 << 20, transcendentals=0),
        name="strip",
    )(place, taps)


def conv_kernel(value, strip_ref, out, stacked, total):
    for e in range(4):
        for b in range(64):
            rows = slice(16 * b, 16 * b + 16)
            cols = slice(256 * e, 256 * e + 256)
            if b - e < 0:
                stacked[rows, cols] = jnp.zeros((16, 256), jnp.bfloat16)
            else:
                j, m = divmod(b - e, 2)
                stacked[rows, cols] = value[j, :, 256 * m : 256 * m + 256]
    for g in range(16):
        taps = jnp.concatenate(
            [strip_ref[:, 256 * (4 * g + e) : 256 * (4 * g + e + 1)] for e in range(4)], axis=0
        )
        term = jnp.dot(stacked[: 1024 - 64 * g], taps, preferred_element_type=jnp.float32)
        if g == 0:
            total[...] = term
        else:
            total[64 * g :] += term
    for b in range(64):
        j, m = divmod(b, 2)
        out[j, :, 256 * m : 256 * m + 256] = total[16 * b : 16 * b + 16].astype(jnp.bfloat16)


def convolve(value, taps_strip):
    vmem = pl.BlockSpec(memory_space=pltpu.VMEM)
    return pl.pallas_call(
        conv_kernel,
        out_shape=jax.ShapeDtypeStruct((32, 16, 512), jnp.bfloat16),
        in_specs=[vmem, vmem],
        out_specs=vmem,
        scratch_shapes=[
            pltpu.VMEM((1024, 1024), jnp.bfloat16),
            pltpu.VMEM((1024, 256), jnp.float32),
        ],
        compiler_params=pltpu.CompilerParams(vmem_limit_bytes=VMEM_LIMIT),
        cost_estimate=pl.CostEstimate(
            flops=4_500_000_000, bytes_accessed=10 << 20, transcendentals=0
        ),
        name="convolve",
    )(value, taps_strip)


def mix_kernel(conv, value, gain, gate, out):
    column = jnp.transpose(jnp.broadcast_to(gain[...], (8, gain.shape[1])))[:, :1]
    total = conv[...].astype(jnp.float32) + column * value[...].astype(jnp.float32)
    out[...] = (gate[...].astype(jnp.float32) * total.T).astype(jnp.bfloat16)


def mix(conv, value, gain, gate):
    return pl.pallas_call(
        mix_kernel,
        out_shape=jax.ShapeDtypeStruct((512, 512), jnp.bfloat16),
        grid=(4,),
        in_specs=[
            pl.BlockSpec((128, 512), lambda i: (i, 0)),
            pl.BlockSpec((128, 512), lambda i: (i, 0)),
            pl.BlockSpec((1, 128), lambda i: (0, i)),
            pl.BlockSpec((512, 128), lambda i: (0, i)),
        ],
        out_specs=pl.BlockSpec((512, 128), lambda i: (0, i)),
        compiler_params=pltpu.CompilerParams(vmem_limit_bytes=VMEM_LIMIT),
        name="mix",
    )(conv, value, gain, gate)


def on_device(hidden, value_weight, gate, filters, skip_gain):
    index = lax.axis_index("seq")
    place = jnp.stack([index // NZ, index % NZ, index // 8]).astype(jnp.int32)
    whole = lax.all_gather(hidden, "tp", axis=1, tiled=True)
    value, taps = gather_and_project(place, whole, value_weight, filters)
    taps = lax.dynamic_index_in_dim(taps, index // 8, 2).astype(jnp.float32)
    taps_strip = strip(place, taps)
    value, taps_strip = lax.optimization_barrier((value, taps_strip))
    moved = lax.all_to_all(value, "seq", split_axis=0, concat_axis=0, tiled=True)
    conv = convolve(moved, taps_strip)
    arrived = lax.all_to_all(conv, "seq", split_axis=0, concat_axis=0, tiled=True)
    return mix(arrived.reshape(512, 512), value.reshape(512, 512), skip_gain[None], gate)


def solution(mesh):
    in_specs = (P("seq", "tp"), P("seq", "tp"), P("seq", "tp"), P("seq", "tp"), P("tp"))
    out_specs = P("seq", "tp")
    return jax.shard_map(
        on_device, mesh=mesh, in_specs=in_specs, out_specs=out_specs, check_vma=False
    )
```

```python
import functools

import jax
import jax.numpy as jnp
from jax import lax
from jax.experimental import pallas as pl
from jax.experimental.pallas import tpu as pltpu
from jax.sharding import PartitionSpec as P

NY, NZ = 4, 8
FIRST = 128
TAP_ROWS = 8
ORDER = (0, 1, 7, 2, 6, 3, 5, 4)
VMEM_LIMIT = 16 * 1024 * 1024


def take_from(array, dy, dz):
    pairs = [
        (((y + dy) % NY) * NZ + (z + dz) % NZ, y * NZ + z) for y in range(NY) for z in range(NZ)
    ]
    return lax.ppermute(array, "seq", pairs)


def starts_kernel(place, out):
    for dy in range(NY):
        for dz in range(NZ):
            block = lax.rem(place[0] + dy, NY) * NZ + lax.rem(place[1] + dz, NZ)
            out[dy * NZ + dz] = block * 2 * FIRST


def starts_of(place):
    return pl.pallas_call(
        starts_kernel,
        out_shape=jax.ShapeDtypeStruct((NY * NZ,), jnp.int32),
        in_specs=[pl.BlockSpec(memory_space=pltpu.SMEM)],
        out_specs=pl.BlockSpec(memory_space=pltpu.SMEM),
        compiler_params=pltpu.CompilerParams(vmem_limit_bytes=VMEM_LIMIT),
        cost_estimate=pl.CostEstimate(
            flops=8_000_000_000, bytes_accessed=1 << 20, transcendentals=0
        ),
        name="starts",
    )(place)


def project_kernel(parts, first, last, starts, hidden, *refs):
    refs = list(refs)
    out = refs.pop()
    total = jnp.zeros((512, 512), jnp.float32) if first else refs.pop()[...]
    pieces = []
    for ref, part in zip(refs, parts, strict=True):
        for at, (dy, dz, second) in enumerate(part):
            start = pl.multiple_of(starts[dy * NZ + dz] + FIRST * second, FIRST)
            pieces.append((start, ref, at))
    for n in range(0, len(pieces), 8):
        group = pieces[n : n + 8]
        left = [hidden[:, pl.ds(start, FIRST)] for start, _, _ in group]
        right = [ref[at, 0:FIRST, :] for _, ref, at in group]
        total += jnp.dot(
            jnp.concatenate(left, axis=1),
            jnp.concatenate(right, axis=0),
            preferred_element_type=jnp.float32,
        )
    out[...] = total.T.reshape(32, 16, 512).astype(jnp.bfloat16) if last else total


def project(starts, hidden, held, before=None, last=False):
    arrays = [array for array, _ in held]
    parts = [part for _, part in held]
    count = sum(len(part) for part in parts)
    shape = (
        jax.ShapeDtypeStruct((32, 16, 512), jnp.bfloat16)
        if last
        else jax.ShapeDtypeStruct((512, 512), jnp.float32)
    )
    vmem = pl.BlockSpec(memory_space=pltpu.VMEM)
    extra = [] if before is None else [before]
    return pl.pallas_call(
        functools.partial(project_kernel, parts, before is None, last),
        out_shape=shape,
        in_specs=[pl.BlockSpec(memory_space=pltpu.SMEM)] + [vmem] * (1 + len(arrays) + len(extra)),
        out_specs=vmem,
        compiler_params=pltpu.CompilerParams(vmem_limit_bytes=VMEM_LIMIT),
        cost_estimate=pl.CostEstimate(
            flops=2 * 512 * 512 * FIRST * count,
            bytes_accessed=count * 256 * 1024,
            transcendentals=0,
        ),
        name=f"project_{count}",
    )(starts, hidden, *arrays, *extra)


def halves(one, other, dy, dz):
    half = one.shape[0] // 2
    return take_from(one[:half], dy, dz), take_from(other[half:], -dy, -dz)


def gather_and_project(place, hidden, weight, filters):
    taps = jnp.tile(filters.T, (TAP_ROWS // filters.shape[1], 1))
    first = jnp.concatenate([weight[:FIRST], taps], axis=0)
    second = weight[FIRST:]
    line = {0: first, 1: take_from(first, 0, 1), -1: take_from(first, 0, -1)}
    column = jnp.stack([second, *(take_from(second, k, 0) for k in (1, 2, 3))])
    line[2], line[-2] = take_from(line[1], 0, 1), take_from(line[-1], 0, -1)
    line[3], line[-3] = take_from(line[2], 0, 1), take_from(line[-2], 0, -1)
    ring = {0: column, 1: take_from(column, 0, 1), -1: take_from(column, 0, -1)}
    line[3], line[-3], ring[1], ring[-1] = lax.optimization_barrier(
        (line[3], line[-3], ring[1], ring[-1])
    )
    line[4] = jnp.concatenate(halves(line[3], line[-3], 0, 1), axis=0)
    mine = jnp.stack([line[k] for k in (0, 1, -1, 2, -2, 3, -3, 4)])
    above, below = take_from(mine, 1, 0), take_from(mine, -1, 0)

    def row(dy, start=0, stop=NZ):
        return [(dy, dz, 0) for dz in ORDER[start:stop]]

    def stack(dz, start=0, stop=NY):
        return [(dy, dz % NZ, 1) for dy in range(start, stop)]

    ring[2], ring[-2] = take_from(ring[1], 0, 1), take_from(ring[-1], 0, -1)
    place, hidden, ring[2], ring[-2] = lax.optimization_barrier(
        (place, hidden, ring[2], ring[-2])
    )
    starts = starts_of(place)
    starts, ring[2], ring[-2] = lax.optimization_barrier((starts, ring[2], ring[-2]))
    held = [(mine, row(0))] + [(ring[k], stack(k)) for k in (0, 1, -1)]
    total = project(starts, hidden, held)
    ring[3], ring[-3] = take_from(ring[2], 0, 1), take_from(ring[-2], 0, -1)
    total = project(starts, hidden, [(ring[k], stack(k)) for k in (2, -2)], total)
    total, above, below = lax.optimization_barrier((total, above, below))
    across = halves(above, below, 1, 0)
    total = project(starts, hidden, [(above, row(1)), (below, row(3))], total)
    total, ring[3], ring[-3] = lax.optimization_barrier((total, ring[3], ring[-3]))
    ends = halves(ring[3], ring[-3], 0, 1)
    total = project(starts, hidden, [(ring[k], stack(k)) for k in (3, -3)], total)
    held = [(across[0], row(2, 0, 4)), (across[1], row(2, 4, 8))]
    held += [(ends[0], stack(4, 0, 2)), (ends[1], stack(4, 2, 4))]
    value = project(starts, hidden, held, total, last=True)
    across = jnp.concatenate([part[:, FIRST:] for part in across], axis=0)
    taps = jnp.stack([mine[:, FIRST:], above[:, FIRST:], across, below[:, FIRST:]])
    return value, taps


def strip_kernel(place, taps, out):
    rows, step = 256, 512
    y, z = place[0], place[1]

    def block(i):
        dy = lax.rem(lax.div(i, NZ) - y + NY, NY)
        dz = lax.rem(lax.rem(i, NZ) - z + NZ, NZ)
        at = jnp.where(dz == 0, 0, jnp.where(dz <= 4, 2 * dz - 1, 16 - 2 * dz))
        return taps[dy, at]

    def chunk(i, carry):
        before = jnp.where(i == 0, 0.0, block(jnp.maximum(i - 1, 0))[:, step - rows :])
        window = jnp.concatenate([before, block(i)], axis=1)
        half = rows // 2
        window = jnp.broadcast_to(window, (half, step + rows))
        rolled = pltpu.roll(window, 0, 1, stride=1, stride_axis=0).astype(jnp.bfloat16)
        start = pl.multiple_of(i * step, step)
        out[:half, pl.ds(start, step)] = rolled[:, rows:]
        out[half:, pl.ds(start, step)] = rolled[:, half : step + half]
        return carry

    lax.fori_loop(0, out.shape[1] // step, chunk, 0, unroll=4)


def strip(place, taps):
    vmem = pl.BlockSpec(memory_space=pltpu.VMEM)
    return pl.pallas_call(
        strip_kernel,
        out_shape=jax.ShapeDtypeStruct((256, 16384), jnp.bfloat16),
        in_specs=[pl.BlockSpec(memory_space=pltpu.SMEM), vmem],
        out_specs=vmem,
        compiler_params=pltpu.CompilerParams(vmem_limit_bytes=VMEM_LIMIT),
        cost_estimate=pl.CostEstimate(flops=10 << 20, bytes_accessed=8 << 20, transcendentals=0),
        name="strip",
    )(place, taps)


def conv_kernel(value, strip_ref, out, stacked, total):
    for e in range(4):
        for b in range(64):
            rows = slice(16 * b, 16 * b + 16)
            cols = slice(256 * e, 256 * e + 256)
            if b - e < 0:
                stacked[rows, cols] = jnp.zeros((16, 256), jnp.bfloat16)
            else:
                j, m = divmod(b - e, 2)
                stacked[rows, cols] = value[j, :, 256 * m : 256 * m + 256]
    for g in range(16):
        taps = jnp.concatenate(
            [strip_ref[:, 256 * (4 * g + e) : 256 * (4 * g + e + 1)] for e in range(4)], axis=0
        )
        term = jnp.dot(stacked[: 1024 - 64 * g], taps, preferred_element_type=jnp.float32)
        if g == 0:
            total[...] = term
        else:
            total[64 * g :] += term
    for b in range(64):
        j, m = divmod(b, 2)
        out[j, :, 256 * m : 256 * m + 256] = total[16 * b : 16 * b + 16].astype(jnp.bfloat16)


def convolve(value, taps_strip):
    vmem = pl.BlockSpec(memory_space=pltpu.VMEM)
    return pl.pallas_call(
        conv_kernel,
        out_shape=jax.ShapeDtypeStruct((32, 16, 512), jnp.bfloat16),
        in_specs=[vmem, vmem],
        out_specs=vmem,
        scratch_shapes=[
            pltpu.VMEM((1024, 1024), jnp.bfloat16),
            pltpu.VMEM((1024, 256), jnp.float32),
        ],
        compiler_params=pltpu.CompilerParams(vmem_limit_bytes=VMEM_LIMIT),
        cost_estimate=pl.CostEstimate(
            flops=4_500_000_000, bytes_accessed=10 << 20, transcendentals=0
        ),
        name="convolve",
    )(value, taps_strip)


def mix_kernel(conv, value, gain, gate, out):
    column = jnp.transpose(jnp.broadcast_to(gain[...], (8, gain.shape[1])))[:, :1]
    total = conv[...].astype(jnp.float32) + column * value[...].astype(jnp.float32)
    out[...] = (gate[...].astype(jnp.float32) * total.T).astype(jnp.bfloat16)


def mix(conv, value, gain, gate):
    return pl.pallas_call(
        mix_kernel,
        out_shape=jax.ShapeDtypeStruct((512, 512), jnp.bfloat16),
        grid=(4,),
        in_specs=[
            pl.BlockSpec((128, 512), lambda i: (i, 0)),
            pl.BlockSpec((128, 512), lambda i: (i, 0)),
            pl.BlockSpec((1, 128), lambda i: (0, i)),
            pl.BlockSpec((512, 128), lambda i: (0, i)),
        ],
        out_specs=pl.BlockSpec((512, 128), lambda i: (0, i)),
        compiler_params=pltpu.CompilerParams(vmem_limit_bytes=VMEM_LIMIT),
        name="mix",
    )(conv, value, gain, gate)


def on_device(hidden, value_weight, gate, filters, skip_gain):
    index = lax.axis_index("seq")
    place = jnp.stack([index // NZ, index % NZ, index // 8]).astype(jnp.int32)
    whole = lax.all_gather(hidden, "tp", axis=1, tiled=True)
    value, taps = gather_and_project(place, whole, value_weight, filters)
    taps = lax.dynamic_index_in_dim(taps, index // 8, 2).astype(jnp.float32)
    taps_strip = strip(place, taps)
    value, taps_strip = lax.optimization_barrier((value, taps_strip))
    moved = lax.all_to_all(value, "seq", split_axis=0, concat_axis=0, tiled=True)
    conv = convolve(moved, taps_strip)
    arrived = lax.all_to_all(conv, "seq", split_axis=0, concat_axis=0, tiled=True)
    return mix(arrived.reshape(512, 512), value.reshape(512, 512), skip_gain[None], gate)


def solution(mesh):
    in_specs = (P("seq", "tp"), P("seq", "tp"), P("seq", "tp"), P("seq", "tp"), P("tp"))
    out_specs = P("seq", "tp")
    return jax.shard_map(
        on_device, mesh=mesh, in_specs=in_specs, out_specs=out_specs, check_vma=False
    )
```

```python
import functools

import jax
import jax.numpy as jnp
from jax import lax
from jax.experimental import pallas as pl
from jax.experimental.pallas import tpu as pltpu
from jax.sharding import PartitionSpec as P

NY, NZ = 4, 8
FIRST = 128
TAP_ROWS = 8
ORDER = (0, 1, 7, 2, 6, 3, 5, 4)
VMEM_LIMIT = 16 * 1024 * 1024


def take_from(array, dy, dz):
    pairs = [
        (((y + dy) % NY) * NZ + (z + dz) % NZ, y * NZ + z) for y in range(NY) for z in range(NZ)
    ]
    return lax.ppermute(array, "seq", pairs)


def starts_kernel(place, out):
    for dy in range(NY):
        for dz in range(NZ):
            block = lax.rem(place[0] + dy, NY) * NZ + lax.rem(place[1] + dz, NZ)
            out[dy * NZ + dz] = block * 2 * FIRST


def starts_of(place):
    return pl.pallas_call(
        starts_kernel,
        out_shape=jax.ShapeDtypeStruct((NY * NZ,), jnp.int32),
        in_specs=[pl.BlockSpec(memory_space=pltpu.SMEM)],
        out_specs=pl.BlockSpec(memory_space=pltpu.SMEM),
        compiler_params=pltpu.CompilerParams(vmem_limit_bytes=VMEM_LIMIT),
        cost_estimate=pl.CostEstimate(
            flops=8_000_000_000, bytes_accessed=1 << 20, transcendentals=0
        ),
        name="starts",
    )(place)


def project_kernel(parts, first, last, starts, hidden, *refs):
    refs = list(refs)
    out = refs.pop()
    total = jnp.zeros((512, 512), jnp.float32) if first else refs.pop()[...]
    pieces = []
    for ref, part in zip(refs, parts, strict=True):
        for at, (dy, dz, second) in enumerate(part):
            start = pl.multiple_of(starts[dy * NZ + dz] + FIRST * second, FIRST)
            pieces.append((start, ref, at))
    for n in range(0, len(pieces), 8):
        group = pieces[n : n + 8]
        left = [hidden[:, pl.ds(start, FIRST)] for start, _, _ in group]
        right = [ref[at, 0:FIRST, :] for _, ref, at in group]
        total += jnp.dot(
            jnp.concatenate(left, axis=1),
            jnp.concatenate(right, axis=0),
            preferred_element_type=jnp.float32,
        )
    out[...] = total.T.reshape(32, 16, 512).astype(jnp.bfloat16) if last else total


def project(starts, hidden, held, before=None, last=False):
    arrays = [array for array, _ in held]
    parts = [part for _, part in held]
    count = sum(len(part) for part in parts)
    shape = (
        jax.ShapeDtypeStruct((32, 16, 512), jnp.bfloat16)
        if last
        else jax.ShapeDtypeStruct((512, 512), jnp.float32)
    )
    vmem = pl.BlockSpec(memory_space=pltpu.VMEM)
    extra = [] if before is None else [before]
    return pl.pallas_call(
        functools.partial(project_kernel, parts, before is None, last),
        out_shape=shape,
        in_specs=[pl.BlockSpec(memory_space=pltpu.SMEM)] + [vmem] * (1 + len(arrays) + len(extra)),
        out_specs=vmem,
        compiler_params=pltpu.CompilerParams(vmem_limit_bytes=VMEM_LIMIT),
        cost_estimate=pl.CostEstimate(
            flops=2 * 512 * 512 * FIRST * count,
            bytes_accessed=count * 256 * 1024,
            transcendentals=0,
        ),
        name=f"project_{count}",
    )(starts, hidden, *arrays, *extra)


def halves(one, other, dy, dz):
    half = one.shape[0] // 2
    return take_from(one[:half], dy, dz), take_from(other[half:], -dy, -dz)


def gather_and_project(place, hidden, weight, filters):
    taps = jnp.tile(filters.T, (TAP_ROWS // filters.shape[1], 1))
    first = jnp.concatenate([weight[:FIRST], taps], axis=0)
    second = weight[FIRST:]
    line = {0: first, 1: take_from(first, 0, 1), -1: take_from(first, 0, -1)}
    column = jnp.stack([second, *(take_from(second, k, 0) for k in (1, 2, 3))])
    line[2], line[-2] = take_from(line[1], 0, 1), take_from(line[-1], 0, -1)
    line[3], line[-3] = take_from(line[2], 0, 1), take_from(line[-2], 0, -1)
    ring = {0: column, 1: take_from(column, 0, 1), -1: take_from(column, 0, -1)}
    line[3], line[-3], ring[1], ring[-1] = lax.optimization_barrier(
        (line[3], line[-3], ring[1], ring[-1])
    )
    line[4] = jnp.concatenate(halves(line[3], line[-3], 0, 1), axis=0)
    mine = jnp.stack([line[k] for k in (0, 1, -1, 2, -2, 3, -3, 4)])
    above, below = take_from(mine, 1, 0), take_from(mine, -1, 0)

    def row(dy, start=0, stop=NZ):
        return [(dy, dz, 0) for dz in ORDER[start:stop]]

    def stack(dz, start=0, stop=NY):
        return [(dy, dz % NZ, 1) for dy in range(start, stop)]

    ring[2], ring[-2] = take_from(ring[1], 0, 1), take_from(ring[-1], 0, -1)
    place, hidden, ring[2], ring[-2] = lax.optimization_barrier(
        (place, hidden, ring[2], ring[-2])
    )
    starts = starts_of(place)
    starts, ring[2], ring[-2] = lax.optimization_barrier((starts, ring[2], ring[-2]))
    held = [(mine, row(0))] + [(ring[k], stack(k)) for k in (0, 1, -1)]
    total = project(starts, hidden, held)
    ring[3], ring[-3] = take_from(ring[2], 0, 1), take_from(ring[-2], 0, -1)
    total = project(starts, hidden, [(ring[k], stack(k)) for k in (2, -2)], total)
    total, above, below = lax.optimization_barrier((total, above, below))
    across = halves(above, below, 1, 0)
    total = project(starts, hidden, [(above, row(1)), (below, row(3))], total)
    total, ring[3], ring[-3] = lax.optimization_barrier((total, ring[3], ring[-3]))
    ends = halves(ring[3], ring[-3], 0, 1)
    total = project(starts, hidden, [(ring[k], stack(k)) for k in (3, -3)], total)
    held = [(across[0], row(2, 0, 4)), (across[1], row(2, 4, 8))]
    held += [(ends[0], stack(4, 0, 2)), (ends[1], stack(4, 2, 4))]
    value = project(starts, hidden, held, total, last=True)
    across = jnp.concatenate([part[:, FIRST:] for part in across], axis=0)
    taps = jnp.stack([mine[:, FIRST:], above[:, FIRST:], across, below[:, FIRST:]])
    return value, taps


def strip_kernel(place, taps, out):
    rows, step = 256, 512
    y, z = place[0], place[1]

    def block(i):
        dy = lax.rem(lax.div(i, NZ) - y + NY, NY)
        dz = lax.rem(lax.rem(i, NZ) - z + NZ, NZ)
        at = jnp.where(dz == 0, 0, jnp.where(dz <= 4, 2 * dz - 1, 16 - 2 * dz))
        return taps[dy, at]

    def chunk(i, carry):
        before = jnp.where(i == 0, 0.0, block(jnp.maximum(i - 1, 0))[:, step - rows :])
        window = jnp.concatenate([before, block(i)], axis=1)
        half = rows // 2
        window = jnp.broadcast_to(window, (half, step + rows))
        rolled = pltpu.roll(window, 0, 1, stride=1, stride_axis=0).astype(jnp.bfloat16)
        start = pl.multiple_of(i * step, step)
        out[:half, pl.ds(start, step)] = rolled[:, rows:]
        out[half:, pl.ds(start, step)] = rolled[:, half : step + half]
        return carry

    lax.fori_loop(0, out.shape[1] // step, chunk, 0, unroll=8)


def strip(place, taps):
    vmem = pl.BlockSpec(memory_space=pltpu.VMEM)
    return pl.pallas_call(
        strip_kernel,
        out_shape=jax.ShapeDtypeStruct((256, 16384), jnp.bfloat16),
        in_specs=[pl.BlockSpec(memory_space=pltpu.SMEM), vmem],
        out_specs=vmem,
        compiler_params=pltpu.CompilerParams(vmem_limit_bytes=VMEM_LIMIT),
        cost_estimate=pl.CostEstimate(flops=10 << 20, bytes_accessed=8 << 20, transcendentals=0),
        name="strip",
    )(place, taps)


def conv_kernel(value, strip_ref, out, stacked, total):
    for e in range(4):
        for b in range(64):
            rows = slice(16 * b, 16 * b + 16)
            cols = slice(256 * e, 256 * e + 256)
            if b - e < 0:
                stacked[rows, cols] = jnp.zeros((16, 256), jnp.bfloat16)
            else:
                j, m = divmod(b - e, 2)
                stacked[rows, cols] = value[j, :, 256 * m : 256 * m + 256]
    for g in range(16):
        taps = jnp.concatenate(
            [strip_ref[:, 256 * (4 * g + e) : 256 * (4 * g + e + 1)] for e in range(4)], axis=0
        )
        term = jnp.dot(stacked[: 1024 - 64 * g], taps, preferred_element_type=jnp.float32)
        if g == 0:
            total[...] = term
        else:
            total[64 * g :] += term
    for b in range(64):
        j, m = divmod(b, 2)
        out[j, :, 256 * m : 256 * m + 256] = total[16 * b : 16 * b + 16].astype(jnp.bfloat16)


def convolve(value, taps_strip):
    vmem = pl.BlockSpec(memory_space=pltpu.VMEM)
    return pl.pallas_call(
        conv_kernel,
        out_shape=jax.ShapeDtypeStruct((32, 16, 512), jnp.bfloat16),
        in_specs=[vmem, vmem],
        out_specs=vmem,
        scratch_shapes=[
            pltpu.VMEM((1024, 1024), jnp.bfloat16),
            pltpu.VMEM((1024, 256), jnp.float32),
        ],
        compiler_params=pltpu.CompilerParams(vmem_limit_bytes=VMEM_LIMIT),
        cost_estimate=pl.CostEstimate(
            flops=4_500_000_000, bytes_accessed=10 << 20, transcendentals=0
        ),
        name="convolve",
    )(value, taps_strip)


def mix_kernel(conv, value, gain, gate, out):
    column = jnp.transpose(jnp.broadcast_to(gain[...], (8, gain.shape[1])))[:, :1]
    total = conv[...].astype(jnp.float32) + column * value[...].astype(jnp.float32)
    out[...] = (gate[...].astype(jnp.float32) * total.T).astype(jnp.bfloat16)


def mix(conv, value, gain, gate):
    return pl.pallas_call(
        mix_kernel,
        out_shape=jax.ShapeDtypeStruct((512, 512), jnp.bfloat16),
        grid=(2,),
        in_specs=[
            pl.BlockSpec((256, 512), lambda i: (i, 0)),
            pl.BlockSpec((256, 512), lambda i: (i, 0)),
            pl.BlockSpec((1, 256), lambda i: (0, i)),
            pl.BlockSpec((512, 256), lambda i: (0, i)),
        ],
        out_specs=pl.BlockSpec((512, 256), lambda i: (0, i)),
        compiler_params=pltpu.CompilerParams(vmem_limit_bytes=VMEM_LIMIT),
        name="mix",
    )(conv, value, gain, gate)


def on_device(hidden, value_weight, gate, filters, skip_gain):
    index = lax.axis_index("seq")
    place = jnp.stack([index // NZ, index % NZ, index // 8]).astype(jnp.int32)
    whole = lax.all_gather(hidden, "tp", axis=1, tiled=True)
    value, taps = gather_and_project(place, whole, value_weight, filters)
    taps = lax.dynamic_index_in_dim(taps, index // 8, 2).astype(jnp.float32)
    taps_strip = strip(place, taps)
    value, taps_strip = lax.optimization_barrier((value, taps_strip))
    moved = lax.all_to_all(value, "seq", split_axis=0, concat_axis=0, tiled=True)
    conv = convolve(moved, taps_strip)
    arrived = lax.all_to_all(conv, "seq", split_axis=0, concat_axis=0, tiled=True)
    return mix(arrived.reshape(512, 512), value.reshape(512, 512), skip_gain[None], gate)


def solution(mesh):
    in_specs = (P("seq", "tp"), P("seq", "tp"), P("seq", "tp"), P("seq", "tp"), P("tp"))
    out_specs = P("seq", "tp")
    return jax.shard_map(
        on_device, mesh=mesh, in_specs=in_specs, out_specs=out_specs, check_vma=False
    )
```

```python
import functools

import jax
import jax.numpy as jnp
from jax import lax
from jax.experimental import pallas as pl
from jax.experimental.pallas import tpu as pltpu
from jax.sharding import PartitionSpec as P

NY, NZ = 4, 8
FIRST = 128
TAP_ROWS = 8
ORDER = (0, 1, 7, 2, 6, 3, 5, 4)
VMEM_LIMIT = 16 * 1024 * 1024


def take_from(array, dy, dz):
    pairs = [
        (((y + dy) % NY) * NZ + (z + dz) % NZ, y * NZ + z) for y in range(NY) for z in range(NZ)
    ]
    return lax.ppermute(array, "seq", pairs)


def starts_kernel(place, out):
    for dy in range(NY):
        for dz in range(NZ):
            block = lax.rem(place[0] + dy, NY) * NZ + lax.rem(place[1] + dz, NZ)
            out[dy * NZ + dz] = block * 2 * FIRST


def starts_of(place):
    return pl.pallas_call(
        starts_kernel,
        out_shape=jax.ShapeDtypeStruct((NY * NZ,), jnp.int32),
        in_specs=[pl.BlockSpec(memory_space=pltpu.SMEM)],
        out_specs=pl.BlockSpec(memory_space=pltpu.SMEM),
        compiler_params=pltpu.CompilerParams(vmem_limit_bytes=VMEM_LIMIT),
        cost_estimate=pl.CostEstimate(
            flops=8_000_000_000, bytes_accessed=1 << 20, transcendentals=0
        ),
        name="starts",
    )(place)


def project_kernel(parts, first, last, starts, hidden, *refs):
    refs = list(refs)
    out = refs.pop()
    total = jnp.zeros((512, 512), jnp.float32) if first else refs.pop()[...]
    pieces = []
    for ref, part in zip(refs, parts, strict=True):
        for at, (dy, dz, second) in enumerate(part):
            start = pl.multiple_of(starts[dy * NZ + dz] + FIRST * second, FIRST)
            pieces.append((start, ref, at))
    for n in range(0, len(pieces), 8):
        group = pieces[n : n + 8]
        left = [hidden[:, pl.ds(start, FIRST)] for start, _, _ in group]
        right = [ref[at, 0:FIRST, :] for _, ref, at in group]
        total += jnp.dot(
            jnp.concatenate(left, axis=1),
            jnp.concatenate(right, axis=0),
            preferred_element_type=jnp.float32,
        )
    out[...] = total.T.reshape(32, 16, 512).astype(jnp.bfloat16) if last else total


def project(starts, hidden, held, before=None, last=False):
    arrays = [array for array, _ in held]
    parts = [part for _, part in held]
    count = sum(len(part) for part in parts)
    shape = (
        jax.ShapeDtypeStruct((32, 16, 512), jnp.bfloat16)
        if last
        else jax.ShapeDtypeStruct((512, 512), jnp.float32)
    )
    vmem = pl.BlockSpec(memory_space=pltpu.VMEM)
    extra = [] if before is None else [before]
    return pl.pallas_call(
        functools.partial(project_kernel, parts, before is None, last),
        out_shape=shape,
        in_specs=[pl.BlockSpec(memory_space=pltpu.SMEM)] + [vmem] * (1 + len(arrays) + len(extra)),
        out_specs=vmem,
        compiler_params=pltpu.CompilerParams(vmem_limit_bytes=VMEM_LIMIT),
        cost_estimate=pl.CostEstimate(
            flops=2 * 512 * 512 * FIRST * count,
            bytes_accessed=count * 256 * 1024,
            transcendentals=0,
        ),
        name=f"project_{count}",
    )(starts, hidden, *arrays, *extra)


def halves(one, other, dy, dz):
    half = one.shape[0] // 2
    return take_from(one[:half], dy, dz), take_from(other[half:], -dy, -dz)


def gather_and_project(place, hidden, weight, filters):
    taps = jnp.tile(filters.T, (TAP_ROWS // filters.shape[1], 1))
    first = jnp.concatenate([weight[:FIRST], taps], axis=0)
    second = weight[FIRST:]
    line = {0: first, 1: take_from(first, 0, 1), -1: take_from(first, 0, -1)}
    column = jnp.stack([second, *(take_from(second, k, 0) for k in (1, 2, 3))])
    line[2], line[-2] = take_from(line[1], 0, 1), take_from(line[-1], 0, -1)
    line[3], line[-3] = take_from(line[2], 0, 1), take_from(line[-2], 0, -1)
    ring = {0: column, 1: take_from(column, 0, 1), -1: take_from(column, 0, -1)}
    line[3], line[-3], ring[1], ring[-1] = lax.optimization_barrier(
        (line[3], line[-3], ring[1], ring[-1])
    )
    line[4] = jnp.concatenate(halves(line[3], line[-3], 0, 1), axis=0)
    mine = jnp.stack([line[k] for k in (0, 1, -1, 2, -2, 3, -3, 4)])
    above, below = take_from(mine, 1, 0), take_from(mine, -1, 0)

    def row(dy, start=0, stop=NZ):
        return [(dy, dz, 0) for dz in ORDER[start:stop]]

    def stack(dz, start=0, stop=NY):
        return [(dy, dz % NZ, 1) for dy in range(start, stop)]

    ring[2], ring[-2] = take_from(ring[1], 0, 1), take_from(ring[-1], 0, -1)
    place, hidden, ring[2], ring[-2] = lax.optimization_barrier(
        (place, hidden, ring[2], ring[-2])
    )
    starts = starts_of(place)
    starts, ring[2], ring[-2] = lax.optimization_barrier((starts, ring[2], ring[-2]))
    held = [(mine, row(0))] + [(ring[k], stack(k)) for k in (0, 1, -1)]
    total = project(starts, hidden, held)
    ring[3], ring[-3] = take_from(ring[2], 0, 1), take_from(ring[-2], 0, -1)
    total = project(starts, hidden, [(ring[k], stack(k)) for k in (2, -2)], total)
    total, above, below = lax.optimization_barrier((total, above, below))
    across = halves(above, below, 1, 0)
    total = project(starts, hidden, [(above, row(1)), (below, row(3))], total)
    ends = halves(ring[3], ring[-3], 0, 1)
    total = project(starts, hidden, [(ring[k], stack(k)) for k in (3, -3)], total)
    held = [(across[0], row(2, 0, 4)), (across[1], row(2, 4, 8))]
    held += [(ends[0], stack(4, 0, 2)), (ends[1], stack(4, 2, 4))]
    value = project(starts, hidden, held, total, last=True)
    across = jnp.concatenate([part[:, FIRST:] for part in across], axis=0)
    taps = jnp.stack([mine[:, FIRST:], above[:, FIRST:], across, below[:, FIRST:]])
    return value, taps


def strip_kernel(place, taps, out):
    rows, step = 256, 512
    y, z = place[0], place[1]

    def block(i):
        dy = lax.rem(lax.div(i, NZ) - y + NY, NY)
        dz = lax.rem(lax.rem(i, NZ) - z + NZ, NZ)
        at = jnp.where(dz == 0, 0, jnp.where(dz <= 4, 2 * dz - 1, 16 - 2 * dz))
        return taps[dy, at]

    def chunk(i, carry):
        before = jnp.where(i == 0, 0.0, block(jnp.maximum(i - 1, 0))[:, step - rows :])
        window = jnp.concatenate([before, block(i)], axis=1)
        half = rows // 2
        window = jnp.broadcast_to(window, (half, step + rows))
        rolled = pltpu.roll(window, 0, 1, stride=1, stride_axis=0).astype(jnp.bfloat16)
        start = pl.multiple_of(i * step, step)
        out[:half, pl.ds(start, step)] = rolled[:, rows:]
        out[half:, pl.ds(start, step)] = rolled[:, half : step + half]
        return carry

    lax.fori_loop(0, out.shape[1] // step, chunk, 0, unroll=8)


def strip(place, taps):
    vmem = pl.BlockSpec(memory_space=pltpu.VMEM)
    return pl.pallas_call(
        strip_kernel,
        out_shape=jax.ShapeDtypeStruct((256, 16384), jnp.bfloat16),
        in_specs=[pl.BlockSpec(memory_space=pltpu.SMEM), vmem],
        out_specs=vmem,
        compiler_params=pltpu.CompilerParams(vmem_limit_bytes=VMEM_LIMIT),
        cost_estimate=pl.CostEstimate(flops=10 << 20, bytes_accessed=8 << 20, transcendentals=0),
        name="strip",
    )(place, taps)


def conv_kernel(value, strip_ref, out, stacked, total):
    for e in range(4):
        for b in range(64):
            rows = slice(16 * b, 16 * b + 16)
            cols = slice(256 * e, 256 * e + 256)
            if b - e < 0:
                stacked[rows, cols] = jnp.zeros((16, 256), jnp.bfloat16)
            else:
                j, m = divmod(b - e, 2)
                stacked[rows, cols] = value[j, :, 256 * m : 256 * m + 256]
    for g in range(16):
        taps = jnp.concatenate(
            [strip_ref[:, 256 * (4 * g + e) : 256 * (4 * g + e + 1)] for e in range(4)], axis=0
        )
        term = jnp.dot(stacked[: 1024 - 64 * g], taps, preferred_element_type=jnp.float32)
        if g == 0:
            total[...] = term
        else:
            total[64 * g :] += term
    for b in range(64):
        j, m = divmod(b, 2)
        out[j, :, 256 * m : 256 * m + 256] = total[16 * b : 16 * b + 16].astype(jnp.bfloat16)


def convolve(value, taps_strip):
    vmem = pl.BlockSpec(memory_space=pltpu.VMEM)
    return pl.pallas_call(
        conv_kernel,
        out_shape=jax.ShapeDtypeStruct((32, 16, 512), jnp.bfloat16),
        in_specs=[vmem, vmem],
        out_specs=vmem,
        scratch_shapes=[
            pltpu.VMEM((1024, 1024), jnp.bfloat16),
            pltpu.VMEM((1024, 256), jnp.float32),
        ],
        compiler_params=pltpu.CompilerParams(vmem_limit_bytes=VMEM_LIMIT),
        cost_estimate=pl.CostEstimate(
            flops=4_500_000_000, bytes_accessed=10 << 20, transcendentals=0
        ),
        name="convolve",
    )(value, taps_strip)


def mix_kernel(conv, value, gain, gate, out):
    column = jnp.transpose(jnp.broadcast_to(gain[...], (8, gain.shape[1])))[:, :1]
    total = conv[...].astype(jnp.float32) + column * value[...].astype(jnp.float32)
    out[...] = (gate[...].astype(jnp.float32) * total.T).astype(jnp.bfloat16)


def mix(conv, value, gain, gate):
    return pl.pallas_call(
        mix_kernel,
        out_shape=jax.ShapeDtypeStruct((512, 512), jnp.bfloat16),
        grid=(2,),
        in_specs=[
            pl.BlockSpec((256, 512), lambda i: (i, 0)),
            pl.BlockSpec((256, 512), lambda i: (i, 0)),
            pl.BlockSpec((1, 256), lambda i: (0, i)),
            pl.BlockSpec((512, 256), lambda i: (0, i)),
        ],
        out_specs=pl.BlockSpec((512, 256), lambda i: (0, i)),
        compiler_params=pltpu.CompilerParams(vmem_limit_bytes=VMEM_LIMIT),
        name="mix",
    )(conv, value, gain, gate)


def on_device(hidden, value_weight, gate, filters, skip_gain):
    index = lax.axis_index("seq")
    place = jnp.stack([index // NZ, index % NZ, index // 8]).astype(jnp.int32)
    whole = lax.all_gather(hidden, "tp", axis=1, tiled=True)
    value, taps = gather_and_project(place, whole, value_weight, filters)
    taps = lax.dynamic_index_in_dim(taps, index // 8, 2).astype(jnp.float32)
    taps_strip = strip(place, taps)
    value, taps_strip = lax.optimization_barrier((value, taps_strip))
    moved = lax.all_to_all(value, "seq", split_axis=0, concat_axis=0, tiled=True)
    conv = convolve(moved, taps_strip)
    arrived = lax.all_to_all(conv, "seq", split_axis=0, concat_axis=0, tiled=True)
    return mix(arrived.reshape(512, 512), value.reshape(512, 512), skip_gain[None], gate)


def solution(mesh):
    in_specs = (P("seq", "tp"), P("seq", "tp"), P("seq", "tp"), P("seq", "tp"), P("tp"))
    out_specs = P("seq", "tp")
    return jax.shard_map(
        on_device, mesh=mesh, in_specs=in_specs, out_specs=out_specs, check_vma=False
    )
```
